256 devices in a mesh: row: 16 (over y, x), col: 16 (over z, core).
Axes of the slice: x: 4, y: 4, z: 8, core: 2. Of those that a mesh axis runs over, the one named last changes fastest.
Arguments:
- block_input: bfloat16 [512, 12288], P('col', 'row'), may hold values from -6 to 6
- out_grad: bfloat16 [512, 12288], P('col', 'row'), may hold values from -6 to 6
- up_weight: bfloat16 [12288, 24576], P('row', 'col'), may hold values from -0.0546875 to 0.0546875
- down_weight: bfloat16 [24576, 12288], P('col', 'row'), may hold values from -0.0390625 to 0.0390625
Outputs:
- block_output: bfloat16 [512, 12288], P('col', 'row')
- input_grad: bfloat16 [512, 12288], P('col', 'row')
- up_grad: bfloat16 [12288, 24576], P('row', 'col')
- down_grad: bfloat16 [24576, 12288], P('col', 'row')
The draws below stay inside these ranges and needn't reach their ends.
All inputs are finite; a program needn't handle non-finite values.
Results may differ from the reference program's by a relative error of at most 0.033.
Values may be sent and summed in bfloat16 or wider, within the bound.
A program may use at most 64 MiB of HBM per device.

```python
import jax
import jax.numpy as jnp
from jax import lax

D = 12288
FF = 24576
TOKENS = 512
N_ROW = 16
N_COL = 16


def block_scale(own_key, extent, split, low, top_value):
    def one(axis_at, shards_of):
        heights = jax.random.uniform(jax.random.fold_in(jax.random.fold_in(own_key, 6), axis_at), (shards_of,), jnp.float32, low / len(split), top_value / len(split))
        return jnp.repeat(jnp.exp(heights), extent[axis_at] // shards_of).reshape((-1,) + (1,) * (len(extent) - axis_at - 1))

    factor_of = one(*split[0])
    for cut in split[1:]:
        factor_of = factor_of * one(*cut)
    return factor_of


def scatter_about(key, dims, width, limit, pieces=(), kind=jnp.bfloat16):
    gain = block_scale(key, dims, pieces, -0.22, 0.18) if pieces else 1.0
    drawn = jax.random.normal(key, dims, jnp.float32) * width * gain
    return jnp.minimum(jnp.maximum(drawn, -limit), limit).astype(kind)


def setup_inputs(seed: int = 0) -> dict:
    arg_keys = jax.random.split(jax.random.key(seed), 5)
    block_input = scatter_about(arg_keys[0], (TOKENS, D), 1.0, 6.0, ((0, 16), (1, 16)))
    out_grad = scatter_about(arg_keys[1], (TOKENS, D), 1.0, 6.0, ((0, 16), (1, 16)))
    up_weight = scatter_about(arg_keys[2], (D, FF), D ** -0.5, 0.0546875, ((0, 16), (1, 16)))
    down_weight = scatter_about(arg_keys[3], (FF, D), FF ** -0.5, 0.0390625, ((0, 16), (1, 16)))
    return {"block_input": block_input, "out_grad": out_grad, "up_weight": up_weight, "down_weight": down_weight}


gelu_c = 0.7978845608028654


def gelu_both(preact):
    cubed = preact * preact * preact
    tanh_term = jnp.tanh(gelu_c * (preact + 0.044715 * cubed))
    value = 0.5 * preact * (1.0 + tanh_term)
    slope = 0.5 * (1.0 + tanh_term) + 0.5 * preact * (1.0 - tanh_term * tanh_term) * gelu_c * (1.0 + 3.0 * 0.044715 * preact * preact)
    return value, slope


def rounded(term):
    return lax.optimization_barrier(term.astype(jnp.bfloat16)).astype(jnp.float32)


def reference(block_input, out_grad, up_weight, down_weight):
    width_d = D // N_ROW
    width_f = FF // N_COL

    def feature_block(block_index, carry):
        pre_acc, grad_acc = carry
        start = (block_index * width_d).astype(jnp.int32)
        input_part = lax.dynamic_slice_in_dim(block_input, start, width_d, 1)
        grad_part = lax.dynamic_slice_in_dim(out_grad, start, width_d, 1)
        up_part = lax.dynamic_slice_in_dim(up_weight, start, width_d, 0)
        down_part = lax.dynamic_slice_in_dim(down_weight, start, width_d, 1)
        forward = jnp.dot(input_part, up_part, preferred_element_type=jnp.float32)
        backward = lax.dot_general(grad_part, down_part, (((1,), (1,)), ((), ())), preferred_element_type=jnp.float32)
        return pre_acc + rounded(forward), grad_acc + rounded(backward)

    zero_f = jnp.zeros((TOKENS, FF), jnp.float32)
    preact, hgrad = lax.fori_loop(0, N_ROW, feature_block, (zero_f, zero_f))
    value, slope = gelu_both(preact)
    hidden = value.astype(jnp.bfloat16)
    act_grad = (hgrad * slope).astype(jnp.bfloat16)

    def hidden_block(block_index, carry):
        out_acc, back_acc = carry
        start = (block_index * width_f).astype(jnp.int32)
        hidden_part = lax.dynamic_slice_in_dim(hidden, start, width_f, 1)
        act_part = lax.dynamic_slice_in_dim(act_grad, start, width_f, 1)
        down_part = lax.dynamic_slice_in_dim(down_weight, start, width_f, 0)
        up_part = lax.dynamic_slice_in_dim(up_weight, start, width_f, 1)
        out_term = jnp.dot(hidden_part, down_part, preferred_element_type=jnp.float32)
        back_term = lax.dot_general(act_part, up_part, (((1,), (1,)), ((), ())), preferred_element_type=jnp.float32)
        return out_acc + rounded(out_term), back_acc + rounded(back_term)

    zero_d = jnp.zeros((TOKENS, D), jnp.float32)
    out_sum, back_sum = lax.fori_loop(0, N_COL, hidden_block, (zero_d, zero_d))
    up_grad = lax.dot_general(block_input, act_grad, (((0,), (0,)), ((), ())), preferred_element_type=jnp.float32)
    down_grad = lax.dot_general(hidden, out_grad, (((0,), (0,)), ((), ())), preferred_element_type=jnp.float32)
    return (out_sum.astype(jnp.bfloat16), back_sum.astype(jnp.bfloat16),
            up_grad.astype(jnp.bfloat16), down_grad.astype(jnp.bfloat16))
```

```python
import functools

import jax
import jax.numpy as jnp
from jax import lax
from jax.experimental import pallas as pl
from jax.experimental.pallas import tpu as pltpu
from jax.sharding import PartitionSpec as P

MESH = pl.DeviceIdType.MESH
gelu_c = 0.7978845608028654
f32 = jnp.float32
bf16 = jnp.bfloat16

NX = 4
NZ = 8
ORDER = (1, -1, 2, -2, 3, -3, 0, 4)
POS = {d: i for i, d in enumerate(ORDER)}
CHUNKS = ((0, 1), (2, 3), (4, 5), (6, 7))
STEP = 1
N_SEMS = 224


def activate(preact, hgrad):
    cubed = preact * preact * preact
    tanh_term = jnp.tanh(gelu_c * (preact + 0.044715 * cubed))
    value = 0.5 * preact * (1.0 + tanh_term)
    slope = 0.5 * (1.0 + tanh_term) + 0.5 * preact * (1.0 - tanh_term * tanh_term) * gelu_c * (
        1.0 + 3.0 * 0.044715 * preact * preact
    )
    return value.astype(bf16), (hgrad * slope).astype(bf16)


def dot(a, b, ca, cb):
    return lax.dot_general(a, b, (((ca,), (cb,)), ((), ())), preferred_element_type=f32)


def kernel(
    x_in, g_in, u_in, d_in,
    out_o, back_o, ug_o, dg_o,
    xg, u, dn, part, hid, via, full, quarter, got, outp, sib, zbuf, small, ug, dg,
    ssem, rsem, lsem,
):
    tb, dk = x_in.shape
    fq = u.shape[2]
    st = 2 * tb
    sub = st // NX
    row, col = lax.axis_index("row"), lax.axis_index("col")
    cx, cy = row % NX, row // NX
    cz, core = col // 2, col % 2

    def device(axis, off):
        if axis == "x":
            return (cy * NX + (cx + off) % NX, col)
        if axis == "y":
            return (((cy + off) % NX) * NX + cx, col)
        if axis == "z":
            return (row, ((cz + off) % NZ) * 2 + core)
        return (row, cz * 2 + 1 - core)

    place = {"x": cx, "y": cy}
    sends = []
    n_local = [0]

    def send(src, dst, target):
        i = len(sends)
        copy = pltpu.make_async_remote_copy(
            src_ref=src, dst_ref=dst, send_sem=ssem.at[i], recv_sem=rsem.at[i],
            device_id=target, device_id_type=MESH,
        )
        copy.start()
        sends.append(copy)
        return copy

    def local(src, dst):
        i = n_local[0]
        n_local[0] += 1
        copy = pltpu.make_async_copy(src, dst, lsem.at[i])
        copy.start()
        return copy

    def rows(pos, first=0, count=st):
        return pl.ds(pos * st + first, count)

    own = [
        local(x_in, xg.at[rows(POS[0], 0, tb), pl.ds(0, dk)]),
        local(g_in, xg.at[rows(POS[0], 0, tb), pl.ds(dk, dk)]),
    ]
    weights = [local(u_in.at[:, pl.ds(q * fq, fq)], u.at[q]) for q in range(NX)]
    weights += [local(d_in.at[pl.ds(q * fq, fq), :], dn.at[q]) for q in range(NX)]

    barrier = pltpu.get_barrier_semaphore()
    partners = [(a, o) for a in "xy" for o in (1, 2, 3)] + [("z", o) for o in range(1, NZ)] + [("c", 1)]
    for axis, off in partners:
        pl.semaphore_signal(barrier, inc=1, device_id=device(axis, off), device_id_type=MESH)
    pl.semaphore_wait(barrier, len(partners))

    arrival, shared = {}, {}

    def pass_on(d, to, cols=None):
        cols = pl.ds(0, 2 * dk) if cols is None else cols
        return send(xg.at[rows(POS[d], 0, tb), cols], xg.at[rows(POS[to], 0, tb), cols],
                    device("z", 1 if to < 0 or (to == 4 and d < 0) else -1))

    def share(d):
        shared[d] = send(xg.at[rows(POS[d], 0, tb)], xg.at[rows(POS[d], tb, tb)], device("c", 1))

    for copy in own:
        copy.wait()
    arrival[-1] = [pass_on(0, -1)]
    arrival[1] = [pass_on(0, 1)]
    share(0)

    def arrive(d):
        for copy in arrival[d]:
            copy.wait_recv()
        if d in (-1, -2):
            arrival[d - 1] = [pass_on(d, d - 1)]
        elif d in (1, 2):
            arrival[d + 1] = [pass_on(d, d + 1)]
        elif d == -3:
            arrival.setdefault(4, []).append(pass_on(d, 4, pl.ds(0, dk)))
        elif d == 3:
            arrival.setdefault(4, []).append(pass_on(d, 4, pl.ds(dk, dk)))
        share(d)

    pend = {}

    def axes(pos):
        return ("x", "y") if pos % 2 == 0 else ("y", "x")

    def first_products(chunk):
        for pos in chunk:
            shared[ORDER[pos]].wait_recv()
        span = pl.ds(chunk[0] * st, len(chunk) * st)
        xs, gs = xg[span, :dk], xg[span, dk:]

        def one(q, _):
            part[q, span, :fq] = dot(xs, u[q], 1, 0).astype(bf16)
            part[q, span, fq:] = dot(gs, dn[q], 1, 1).astype(bf16)
            return 0

        lax.fori_loop(0, NX, one, 0)
        for pos in chunk:
            a1, _ = axes(pos)
            far = (place[a1] + 2) % NX
            pend[pos] = [
                send(part.at[far, rows(pos), pl.ds(0, fq)], via.at[0, pos], device(a1, 1)),
                send(part.at[far, rows(pos), pl.ds(fq, fq)], via.at[1, pos], device(a1, -1)),
            ]

    def first_sum(chunk):
        for pos in chunk:
            a1, _ = axes(pos)
            right, left = (place[a1] + 1) % NX, (place[a1] + NX - 1) % NX
            pend[pos][0].wait_recv()
            part[right, rows(pos), :fq] = (
                part[right, rows(pos), :fq].astype(f32) + via[0, pos].astype(f32)
            ).astype(bf16)
            to_right = send(part.at[right, rows(pos)], full.at[0, pos], device(a1, 1))
            pend[pos][1].wait_recv()
            part[left, rows(pos), fq:] = (
                part[left, rows(pos), fq:].astype(f32) + via[1, pos].astype(f32)
            ).astype(bf16)
            pend[pos] = [to_right, send(part.at[left, rows(pos)], full.at[1, pos], device(a1, -1))]

    def second_sum(chunk):
        for pos in chunk:
            a1, a2 = axes(pos)
            for copy in pend[pos]:
                copy.wait_recv()
            total = (
                part[place[a1], rows(pos), :].astype(f32) + full[0, pos].astype(f32) + full[1, pos].astype(f32)
            ).astype(bf16)
            for k in range(NX):
                quarter[pos, k] = total[k * sub:(k + 1) * sub]
            pend[pos] = [
                send(quarter.at[pos, (place[a2] + o) % NX], got.at[pos, o - 1], device(a2, o)) for o in (1, 3, 2)
            ]

    def act(chunk):
        for pos in chunk:
            a1, a2 = axes(pos)
            for copy in pend[pos]:
                copy.wait_recv()
            total = quarter[pos, place[a2]].astype(f32)
            for o in range(NX - 1):
                total = total + got[pos, o].astype(f32)
            value, grad = activate(total[:, :fq], total[:, fq:])
            mine = pl.ds(pl.multiple_of(pos * st + place[a2] * sub, sub), sub)
            hid[place[a1], mine, :fq] = value
            hid[place[a1], mine, fq:] = grad
            block = hid.at[place[a1], mine]
            pend[pos] = [send(block, block, device(a2, o)) for o in (1, 3, 2)]

    def gather(chunk):
        for pos in chunk:
            a1, _ = axes(pos)
            for copy in pend[pos]:
                copy.wait_recv()
            block = hid.at[place[a1], rows(pos)]
            pend[pos] = [send(block, block, device(a1, 1)), send(block, block, device(a1, -1))]

    def forward(chunk):
        for pos in chunk:
            a1, _ = axes(pos)
            right, left = (place[a1] + 1) % NX, (place[a1] + NX - 1) % NX
            pend[pos][0].wait_recv()
            block = hid.at[left, rows(pos), pl.ds(0, fq)]
            to_right = send(block, block, device(a1, 1))
            pend[pos][1].wait_recv()
            block = hid.at[right, rows(pos), pl.ds(fq, fq)]
            pend[pos] = [to_right, send(block, block, device(a1, -1))]

    def second_products(chunk):
        for pos in chunk:
            for copy in pend[pos]:
                copy.wait_recv()
        span = pl.ds(chunk[0] * st, len(chunk) * st)
        out = dot(hid[0, span, :fq], dn[0], 1, 0)
        for q in range(1, NX):
            out = out + dot(hid[q, span, :fq], dn[q], 1, 0)
        outp[span, :dk] = out.astype(bf16)
        back = dot(hid[0, span, fq:], u[0], 1, 1)
        for q in range(1, NX):
            back = back + dot(hid[q, span, fq:], u[q], 1, 1)
        outp[span, dk:] = back.astype(bf16)
        for pos in chunk:
            pend[pos] = [send(outp.at[rows(pos, tb, tb)], sib.at[pos], device("c", 1))]

    landed = []

    def both_cores(chunk):
        for pos in chunk:
            pend[pos][0].wait_recv()
            mine = rows(pos, 0, tb)
            outp[mine, :] = (outp[mine, :].astype(f32) + sib[pos].astype(f32)).astype(bf16)
            d = ORDER[pos]
            if d:
                landed.append(send(outp.at[mine], zbuf.at[pos], device("z", d)))

    stages = [first_products, first_sum, second_sum, act, gather, forward, second_products, both_cores]
    for tick in range(len(stages) + STEP * (len(CHUNKS) - 1)):
        for k in range(len(CHUNKS)):
            s = tick - STEP * k
            if s == 0:
                if k == 0:
                    for copy in weights:
                        copy.wait()
                for pos in CHUNKS[k]:
                    if ORDER[pos]:
                        arrive(ORDER[pos])
            if 0 <= s < len(stages):
                stages[s](CHUNKS[k])

    def weight_grads(q, _):
        ug[q] = dot(xg[:, :dk], hid[q, :, fq:], 0, 0).astype(bf16)
        pltpu.make_async_copy(ug.at[q], ug_o.at[:, pl.ds(pl.multiple_of(q * fq, 128), fq)], lsem.at[16 + q]).start()
        dg[q] = dot(hid[q, :, :fq], xg[:, dk:], 0, 0).astype(bf16)
        pltpu.make_async_copy(dg.at[q], dg_o.at[pl.ds(pl.multiple_of(q * fq, 128), fq), :], lsem.at[20 + q]).start()
        return 0

    lax.fori_loop(0, NX, weight_grads, 0)

    for copy in landed:
        copy.wait_recv()
    total = outp[rows(POS[0], 0, tb), :].astype(f32)
    for d in ORDER:
        if d:
            total = total + zbuf[POS[d]].astype(f32)
    small[...] = total.astype(bf16)
    finals = [local(small.at[:, pl.ds(0, dk)], out_o), local(small.at[:, pl.ds(dk, dk)], back_o)]
    for copy in sends:
        copy.wait_send()
    for copy in finals:
        copy.wait()
    for q in range(NX):
        pltpu.make_async_copy(ug.at[q], ug_o.at[:, pl.ds(q * fq, fq)], lsem.at[16 + q]).wait()
        pltpu.make_async_copy(dg.at[q], dg_o.at[pl.ds(q * fq, fq), :], lsem.at[20 + q]).wait()


def body(block_input, out_grad, up_weight, down_weight):
    tb, dk = block_input.shape
    f = up_weight.shape[1]
    fq, st, n = f // NX, 2 * tb, NZ
    anywhere = pl.BlockSpec(memory_space=pl.ANY)
    vm = lambda *shape: pltpu.VMEM(shape, bf16)
    return pl.pallas_call(
        kernel,
        name="block",
        out_shape=(
            jax.ShapeDtypeStruct((tb, dk), bf16),
            jax.ShapeDtypeStruct((tb, dk), bf16),
            jax.ShapeDtypeStruct((dk, f), bf16),
            jax.ShapeDtypeStruct((f, dk), bf16),
        ),
        in_specs=[anywhere] * 4,
        out_specs=(anywhere,) * 4,
        scratch_shapes=[
            vm(n * st, 2 * dk),
            vm(NX, dk, fq),
            vm(NX, fq, dk),
            vm(NX, n * st, 2 * fq),
            vm(NX, n * st, 2 * fq),
            vm(2, n, st, fq),
            vm(2, n, st, 2 * fq),
            vm(n, NX, st // NX, 2 * fq),
            vm(n, NX - 1, st // NX, 2 * fq),
            vm(n * st, 2 * dk),
            vm(n, tb, 2 * dk),
            vm(n, tb, 2 * dk),
            vm(tb, 2 * dk),
            vm(NX, dk, fq),
            vm(NX, fq, dk),
            pltpu.SemaphoreType.DMA((N_SEMS,)),
            pltpu.SemaphoreType.DMA((N_SEMS,)),
            pltpu.SemaphoreType.DMA((24,)),
        ],
        compiler_params=pltpu.CompilerParams(
            collective_id=0, has_side_effects=True, vmem_limit_bytes=56 * 2**20
        ),
        cost_estimate=pl.CostEstimate(flops=12 * n * st * dk * f, bytes_accessed=8 * dk * f, transcendentals=0),
    )(block_input, out_grad, up_weight, down_weight)


def solution(mesh):
    return jax.shard_map(
        body,
        mesh=mesh,
        in_specs=(P("col", "row"), P("col", "row"), P("row", "col"), P("col", "row")),
        out_specs=(P("col", "row"), P("col", "row"), P("row", "col"), P("col", "row")),
        check_vma=False,
    )
```

```python
import functools

import jax
import jax.numpy as jnp
from jax import lax
from jax.experimental import pallas as pl
from jax.experimental.pallas import tpu as pltpu
from jax.sharding import PartitionSpec as P

MESH = pl.DeviceIdType.MESH
gelu_c = 0.7978845608028654
f32 = jnp.float32
bf16 = jnp.bfloat16

NX = 4
NZ = 8
ORDER = (0, 2, -2, 3, -3, 4, 1, -1)
ZSLOT = {1: 0, -1: 1, 2: 2, -2: 3}
POS = {d: i for i, d in enumerate(ORDER)}
CHUNKS = ((0,), (1, 2), (3, 4), (5,), (6, 7))
SCHEDULE = (
    ("p1", 0), ("arr", 1), ("arr", -1), ("p1", 4), ("arr", -2), ("arr", 2), ("s1", 0), ("p1", 1),
    ("arr", -3), ("arr", 3), ("s1", 7), ("s1", 6), ("p1", 2), ("arr", 4), ("s2", 7), ("s1", 1),
    ("p1", 3), ("s1", 4), ("s1", 3), ("s1", 2), ("s2", 6), ("s1", 5), ("s2", 1), ("s3", 7),
    ("s2", 4), ("s2", 3), ("s2", 2), ("s2", 0), ("s3", 6), ("s2", 5), ("s3", 4), ("s4", 7),
    ("s3", 3), ("s3", 1), ("s3", 0), ("s3", 2), ("s3", 5), ("s4", 4), ("s4", 3), ("s4", 6),
    ("s4", 5), ("s5", 4), ("s4", 2), ("s5", 3), ("s5", 5), ("s4", 0), ("s4", 1), ("s5", 7),
    ("s5", 6), ("s5", 2), ("p2", 2), ("p2", 3), ("s6", 3), ("s5", 1), ("s6", 5), ("s6", 4),
    ("s5", 0), ("p2", 4), ("p2", 1), ("s6", 6), ("s6", 7), ("p2", 0), ("s6", 1), ("s6", 2),
    ("s6", 0), ("dw", 0),
)
N_SEMS = 224


def activate(preact, hgrad):
    cubed = preact * preact * preact
    tanh_term = jnp.tanh(gelu_c * (preact + 0.044715 * cubed))
    value = 0.5 * preact * (1.0 + tanh_term)
    slope = 0.5 * (1.0 + tanh_term) + 0.5 * preact * (1.0 - tanh_term * tanh_term) * gelu_c * (
        1.0 + 3.0 * 0.044715 * preact * preact
    )
    return value.astype(bf16), (hgrad * slope).astype(bf16)


def dot(a, b, ca, cb):
    return lax.dot_general(a, b, (((ca,), (cb,)), ((), ())), preferred_element_type=f32)


def kernel(
    x_in, g_in, u_in, d_in,
    out_o, back_o, ug_o, dg_o,
    xg, u, dn, part, hid, via, full, quarter, got, outp, sib, zbuf, mid, mid4, small, ug, dg,
    ssem, rsem, lsem,
):
    tb, dk = x_in.shape
    fq = u.shape[2]
    st = 2 * tb
    sub = st // NX
    row, col = lax.axis_index("row"), lax.axis_index("col")
    cx, cy = row % NX, row // NX
    cz, core = col // 2, col % 2

    def device(axis, off):
        if axis == "x":
            return (cy * NX + (cx + off) % NX, col)
        if axis == "y":
            return (((cy + off) % NX) * NX + cx, col)
        if axis == "z":
            return (row, ((cz + off) % NZ) * 2 + core)
        return (row, cz * 2 + 1 - core)

    place = {"x": cx, "y": cy}
    sends = []
    n_local = [0]

    def send(src, dst, target):
        i = len(sends)
        copy = pltpu.make_async_remote_copy(
            src_ref=src, dst_ref=dst, send_sem=ssem.at[i], recv_sem=rsem.at[i],
            device_id=target, device_id_type=MESH,
        )
        copy.start()
        sends.append(copy)
        return copy

    def local(src, dst):
        i = n_local[0]
        n_local[0] += 1
        copy = pltpu.make_async_copy(src, dst, lsem.at[i])
        copy.start()
        return copy

    def rows(pos, first=0, count=st):
        return pl.ds(pos * st + first, count)

    own = [
        local(x_in, xg.at[rows(POS[0], 0, tb), pl.ds(0, dk)]),
        local(g_in, xg.at[rows(POS[0], 0, tb), pl.ds(dk, dk)]),
    ]
    weights = [local(u_in.at[:, pl.ds(q * fq, fq)], u.at[q]) for q in range(NX)]
    weights += [local(d_in.at[pl.ds(q * fq, fq), :], dn.at[q]) for q in range(NX)]

    barrier = pltpu.get_barrier_semaphore()
    partners = [(a, o) for a in "xy" for o in (1, 2, 3)] + [("z", o) for o in range(1, NZ)] + [("c", 1)]
    for axis, off in partners:
        pl.semaphore_signal(barrier, inc=1, device_id=device(axis, off), device_id_type=MESH)
    pl.semaphore_wait(barrier, len(partners))

    arrival, shared = {}, {}

    def pass_on(d, to, off, cols=None):
        cols = pl.ds(0, 2 * dk) if cols is None else cols
        copy = send(xg.at[rows(POS[d], 0, tb), cols], xg.at[rows(POS[to], 0, tb), cols], device("z", off))
        arrival.setdefault(to, []).append(copy)

    def share(d):
        shared[d] = send(xg.at[rows(POS[d], 0, tb)], xg.at[rows(POS[d], tb, tb)], device("c", 1))

    for copy in own:
        copy.wait()
    pass_on(0, -1, 1)
    pass_on(0, 1, -1)
    share(0)
    pass_on(0, -2, 2)
    pass_on(0, 2, -2)

    def arrive(d):
        for copy in arrival[d]:
            copy.wait_recv()
        if d in (1, -1):
            pass_on(d, 3 * d, -2 * d)
        elif d == -2:
            pass_on(d, 4, 2, pl.ds(0, dk))
        elif d == 2:
            pass_on(d, 4, -2, pl.ds(dk, dk))
        share(d)

    pend, first = {}, {}
    low, high = pl.ds(0, fq), pl.ds(fq, fq)

    def axes(pos):
        return ("x", "y") if pos % 2 == 0 else ("y", "x")

    def first_products(chunk):
        for pos in chunk:
            shared[ORDER[pos]].wait_recv()
        span = pl.ds(chunk[0] * st, len(chunk) * st)
        xs, gs = xg[span, :dk], xg[span, dk:]

        def one(q, _):
            part[q, span, :fq] = dot(xs, u[q], 1, 0).astype(bf16)
            part[q, span, fq:] = dot(gs, dn[q], 1, 1).astype(bf16)
            return 0

        lax.fori_loop(0, NX, one, 0)
        for pos in chunk:
            a1, _ = axes(pos)
            far = (place[a1] + 2) % NX
            right, left = (place[a1] + 1) % NX, (place[a1] + NX - 1) % NX
            first[pos] = [
                send(part.at[far, rows(pos), low], via.at[0, pos], device(a1, 1)),
                send(part.at[far, rows(pos), high], via.at[1, pos], device(a1, -1)),
            ]
            pend[pos] = [
                send(part.at[right, rows(pos), high], full.at[0, pos, :, high], device(a1, 1)),
                send(part.at[left, rows(pos), low], full.at[1, pos, :, low], device(a1, -1)),
            ]

    def first_sum(pos):
        a1, _ = axes(pos)
        right, left = (place[a1] + 1) % NX, (place[a1] + NX - 1) % NX
        first[pos][0].wait_recv()
        part[right, rows(pos), :fq] = (
            part[right, rows(pos), :fq].astype(f32) + via[0, pos].astype(f32)
        ).astype(bf16)
        pend[pos].append(send(part.at[right, rows(pos), low], full.at[0, pos, :, low], device(a1, 1)))
        first[pos][1].wait_recv()
        part[left, rows(pos), fq:] = (
            part[left, rows(pos), fq:].astype(f32) + via[1, pos].astype(f32)
        ).astype(bf16)
        pend[pos].append(send(part.at[left, rows(pos), high], full.at[1, pos, :, high], device(a1, -1)))

    def second_sum(pos):
        a1, a2 = axes(pos)
        for copy in pend[pos]:
            copy.wait_recv()
        total = (
            part[place[a1], rows(pos), :].astype(f32) + full[0, pos].astype(f32) + full[1, pos].astype(f32)
        ).astype(bf16)
        for k in range(NX):
            quarter[pos, k] = total[k * sub:(k + 1) * sub]
        pend[pos] = [
            send(quarter.at[pos, (place[a2] + o) % NX], got.at[pos, o - 1], device(a2, o)) for o in (1, 3, 2)
        ]

    def act(pos):
        a1, a2 = axes(pos)
        for copy in pend[pos]:
            copy.wait_recv()
        total = quarter[pos, place[a2]].astype(f32)
        for o in range(NX - 1):
            total = total + got[pos, o].astype(f32)
        value, grad = activate(total[:, :fq], total[:, fq:])
        mine = pl.ds(pl.multiple_of(pos * st + place[a2] * sub, sub), sub)
        hid[place[a1], mine, :fq] = value
        hid[place[a1], mine, fq:] = grad
        block = hid.at[place[a1], mine]
        pend[pos] = [send(block, block, device(a2, o)) for o in (1, 3, 2)]

    def gather(pos):
        a1, _ = axes(pos)
        for copy in pend[pos]:
            copy.wait_recv()
        h = hid.at[place[a1], rows(pos), low]
        a = hid.at[place[a1], rows(pos), high]
        first[pos] = [send(h, h, device(a1, 1)), send(a, a, device(a1, -1))]
        pend[pos] = [send(a, a, device(a1, 1)), send(h, h, device(a1, -1))]

    def forward(pos):
        a1, _ = axes(pos)
        right, left = (place[a1] + 1) % NX, (place[a1] + NX - 1) % NX
        first[pos][0].wait_recv()
        block = hid.at[left, rows(pos), low]
        pend[pos].append(send(block, block, device(a1, 1)))
        first[pos][1].wait_recv()
        block = hid.at[right, rows(pos), high]
        pend[pos].append(send(block, block, device(a1, -1)))

    def second_products(chunk):
        for pos in chunk:
            for copy in pend[pos]:
                copy.wait_recv()
        span = pl.ds(chunk[0] * st, len(chunk) * st)
        out = dot(hid[0, span, :fq], dn[0], 1, 0)
        for q in range(1, NX):
            out = out + dot(hid[q, span, :fq], dn[q], 1, 0)
        outp[span, :dk] = out.astype(bf16)
        back = dot(hid[0, span, fq:], u[0], 1, 1)
        for q in range(1, NX):
            back = back + dot(hid[q, span, fq:], u[q], 1, 1)
        outp[span, dk:] = back.astype(bf16)
        for pos in chunk:
            pend[pos] = [send(outp.at[rows(pos, tb, tb)], sib.at[pos], device("c", 1))]

    landed = []

    def both_cores(pos):
        pend[pos][0].wait_recv()
        mine = rows(pos, 0, tb)
        total = outp[mine, :].astype(f32) + sib[pos].astype(f32)
        d = ORDER[pos]
        if d in (2, -2):
            side = 0 if d > 0 else 1
            far[3 if d > 0 else -3].wait_recv()
            far[4][side].wait_recv()
            total = total + mid[side].astype(f32)
            cols = slice(side * dk, side * dk + dk)
            outp[mine, :] = total.astype(bf16)
            outp[mine, cols] = (total[:, cols] + mid4[side].astype(f32)).astype(bf16)
        else:
            outp[mine, :] = total.astype(bf16)
        if d in (3, -3):
            far[d] = send(outp.at[mine], mid.at[0 if d > 0 else 1], device("z", d // 3))
        elif d == 4:
            far[4] = [
                send(outp.at[mine, pl.ds(0, dk)], mid4.at[0], device("z", 2)),
                send(outp.at[mine, pl.ds(dk, dk)], mid4.at[1], device("z", -2)),
            ]
        elif d:
            landed[d] = send(outp.at[mine], zbuf.at[ZSLOT[d]], device("z", d))

    far, landed = {}, {}

    def weight_grads(q, _):
        ug[q] = dot(xg[:, :dk], hid[q, :, fq:], 0, 0).astype(bf16)
        pltpu.make_async_copy(ug.at[q], ug_o.at[:, pl.ds(pl.multiple_of(q * fq, 128), fq)], lsem.at[16 + q]).start()
        dg[q] = dot(hid[q, :, :fq], xg[:, dk:], 0, 0).astype(bf16)
        pltpu.make_async_copy(dg.at[q], dg_o.at[pl.ds(pl.multiple_of(q * fq, 128), fq), :], lsem.at[20 + q]).start()
        return 0

    def all_weight_grads(_):
        lax.fori_loop(0, NX, weight_grads, 0)

    steps = {
        "arr": arrive, "p1": first_products, "s1": first_sum, "s2": second_sum, "s3": act, "s4": gather,
        "s5": forward, "p2": second_products, "s6": both_cores, "dw": all_weight_grads,
    }
    for copy in weights:
        copy.wait()
    for name, number in SCHEDULE:
        steps[name](CHUNKS[number] if name in ("p1", "p2") else number)

    total = outp[rows(POS[0], 0, tb), :].astype(f32)
    for d in (1, -1, 2, -2):
        landed[d].wait_recv()
        total = total + zbuf[ZSLOT[d]].astype(f32)
    small[...] = total.astype(bf16)
    finals = [local(small.at[:, pl.ds(0, dk)], out_o), local(small.at[:, pl.ds(dk, dk)], back_o)]
    for copy in sends:
        copy.wait_send()
    for copy in finals:
        copy.wait()
    for q in range(NX):
        pltpu.make_async_copy(ug.at[q], ug_o.at[:, pl.ds(q * fq, fq)], lsem.at[16 + q]).wait()
        pltpu.make_async_copy(dg.at[q], dg_o.at[pl.ds(q * fq, fq), :], lsem.at[20 + q]).wait()


CUTS = 4


def settle_kernel(*refs):
    n = (len(refs) - 2) // 3
    sources, results, held = refs[:n], refs[n:2 * n], refs[2 * n:3 * n]
    load_sem, store_sem = refs[-2:]
    moves = []
    for i in range(n):
        count = sources[i].shape[0]
        cuts = CUTS if count > 64 else 1
        for c in range(cuts):
            part = pl.ds(c * (count // cuts), count // cuts)
            load = pltpu.make_async_copy(sources[i].at[part], held[i].at[part], load_sem.at[i, c])
            store = pltpu.make_async_copy(held[i].at[part], results[i].at[part], store_sem.at[i, c])
            load.start()
            moves.append((load, store))
    for load, store in moves:
        load.wait()
        store.start()
    for _, store in moves:
        store.wait()


def settle(*arrays):
    anywhere = pl.BlockSpec(memory_space=pl.ANY)
    n = len(arrays)
    return pl.pallas_call(
        settle_kernel,
        name="settle",
        out_shape=tuple(jax.ShapeDtypeStruct(a.shape, a.dtype) for a in arrays),
        in_specs=[anywhere] * n,
        out_specs=(anywhere,) * n,
        scratch_shapes=[pltpu.VMEM(a.shape, a.dtype) for a in arrays]
        + [pltpu.SemaphoreType.DMA((n, CUTS)), pltpu.SemaphoreType.DMA((n, CUTS))],
        compiler_params=pltpu.CompilerParams(vmem_limit_bytes=56 * 2**20),
    )(*arrays)


def body(block_input, out_grad, up_weight, down_weight):
    tb, dk = block_input.shape
    f = up_weight.shape[1]
    fq, st, n = f // NX, 2 * tb, NZ
    anywhere = pl.BlockSpec(memory_space=pl.ANY)
    vm = lambda *shape: pltpu.VMEM(shape, bf16)
    results = pl.pallas_call(
        kernel,
        name="block",
        out_shape=(
            jax.ShapeDtypeStruct((tb, dk), bf16),
            jax.ShapeDtypeStruct((tb, dk), bf16),
            jax.ShapeDtypeStruct((dk, f), bf16),
            jax.ShapeDtypeStruct((f, dk), bf16),
        ),
        in_specs=[anywhere] * 4,
        out_specs=(anywhere,) * 4,
        scratch_shapes=[
            vm(n * st, 2 * dk),
            vm(NX, dk, fq),
            vm(NX, fq, dk),
            vm(NX, n * st, 2 * fq),
            vm(NX, n * st, 2 * fq),
            vm(2, n, st, fq),
            vm(2, n, st, 2 * fq),
            vm(n, NX, st // NX, 2 * fq),
            vm(n, NX - 1, st // NX, 2 * fq),
            vm(n * st, 2 * dk),
            vm(n, tb, 2 * dk),
            vm(4, tb, 2 * dk),
        vm(2, tb, 2 * dk),
        vm(2, tb, dk),
            vm(tb, 2 * dk),
            vm(NX, dk, fq),
            vm(NX, fq, dk),
            pltpu.SemaphoreType.DMA((N_SEMS,)),
            pltpu.SemaphoreType.DMA((N_SEMS,)),
            pltpu.SemaphoreType.DMA((24,)),
        ],
        compiler_params=pltpu.CompilerParams(
            collective_id=0, has_side_effects=True, vmem_limit_bytes=56 * 2**20
        ),
        cost_estimate=pl.CostEstimate(flops=12 * n * st * dk * f, bytes_accessed=8 * dk * f, transcendentals=0),
    )(block_input, out_grad, up_weight, down_weight)
    return settle(*results)


def solution(mesh):
    return jax.shard_map(
        body,
        mesh=mesh,
        in_specs=(P("col", "row"), P("col", "row"), P("row", "col"), P("col", "row")),
        out_specs=(P("col", "row"), P("col", "row"), P("row", "col"), P("col", "row")),
        check_vma=False,
    )
```

```python
import functools

import jax
import jax.numpy as jnp
from jax import lax
from jax.experimental import pallas as pl
from jax.experimental.pallas import tpu as pltpu
from jax.sharding import PartitionSpec as P

MESH = pl.DeviceIdType.MESH
gelu_c = 0.7978845608028654
f32 = jnp.float32
bf16 = jnp.bfloat16

NX = 4
NZ = 8
ORDER = (0, 1, -1, 2, -2, 3, -3, 4)
Y_FIRST = (1, 2, 5, 7)
ZSLOT = {1: 0, -1: 1, 2: 2, -2: 3}
POS = {d: i for i, d in enumerate(ORDER)}
SCHEDULE = (
    ("tr", 0), ("aa", 1), ("aa", -1), ("p1", 0), ("arr", 1), ("arr", -1), ("aa", 2), ("p1", 1),
    ("aa", -2), ("pb", 0), ("arr", 2), ("p1", 2), ("arr", -2), ("s1", 0), ("pb", 2), ("pb", 1),
    ("p1", 3), ("pb", 3), ("s1", 1), ("aa", -3), ("aa", 3), ("p1", 4), ("arr", 3), ("arr", -3),
    ("p1", 5), ("p1", 6), ("s1", 2), ("pb", 6), ("pb", 5), ("arr", 4), ("pb", 4), ("p1", 7),
    ("s1", 6), ("s1", 3), ("s1", 5), ("pb", 7), ("s1", 4), ("s2", 1), ("s1", 7), ("s2", 6),
    ("s2", 5), ("s2", 2), ("s2", 4), ("s2", 3), ("s2", 7), ("s3", 6), ("s2", 0), ("s3", 5),
    ("s3", 1), ("s3", 4), ("s3", 7), ("s3", 3), ("s4", 6), ("s4", 5), ("s4", 4), ("s4", 7),
    ("s5", 6), ("s4", 3), ("s3", 2), ("s5", 5), ("s5", 7), ("s4", 1), ("s5", 4), ("s3", 0),
    ("p2", 6), ("s5", 3), ("p2", 5), ("s6", 6), ("p2", 7), ("s5", 1), ("s6", 7), ("s4", 2),
    ("s6", 5), ("s4", 0), ("p2", 4), ("p2", 1), ("s5", 2), ("p2", 3), ("s6", 1), ("s5", 0),
    ("s6", 4), ("s6", 3), ("p2", 2), ("dw", 0), ("s6", 2), ("p2", 0), ("dw", 1), ("dw", 2),
    ("s6", 0), ("dw", 3),
)
N_SEMS = 224


def activate(preact, hgrad):
    cubed = preact * preact * preact
    tanh_term = jnp.tanh(gelu_c * (preact + 0.044715 * cubed))
    value = 0.5 * preact * (1.0 + tanh_term)
    slope = 0.5 * (1.0 + tanh_term) + 0.5 * preact * (1.0 - tanh_term * tanh_term) * gelu_c * (
        1.0 + 3.0 * 0.044715 * preact * preact
    )
    return value.astype(bf16), (hgrad * slope).astype(bf16)


def dot(a, b, ca, cb):
    return lax.dot_general(a, b, (((ca,), (cb,)), ((), ())), preferred_element_type=f32)


def kernel(
    x_in, g_in, u_in, d_in,
    out_o, back_o, ug_o, dg_o,
    xg, u, dn, ut, dt, part, hid, via, full, quarter, got, outp, sib, zbuf, mid, mid4,
    ssem, rsem, lsem,
):
    tb, dk = x_in.shape
    fq = u.shape[2]
    st = 2 * tb
    sub = st // NX
    row, col = lax.axis_index("row"), lax.axis_index("col")
    cx, cy = row % NX, row // NX
    cz, core = col // 2, col % 2

    def device(axis, off):
        if axis == "x":
            return (cy * NX + (cx + off) % NX, col)
        if axis == "y":
            return (((cy + off) % NX) * NX + cx, col)
        if axis == "z":
            return (row, ((cz + off + NZ) % NZ) * 2 + core)
        return (row, cz * 2 + 1 - core)

    place = {"x": cx, "y": cy}
    sends = []
    n_local = [0]

    def send(src, dst, target):
        i = len(sends)
        copy = pltpu.make_async_remote_copy(
            src_ref=src, dst_ref=dst, send_sem=ssem.at[i], recv_sem=rsem.at[i],
            device_id=target, device_id_type=MESH,
        )
        copy.start()
        sends.append(copy)
        return copy

    def local(src, dst):
        i = n_local[0]
        n_local[0] += 1
        copy = pltpu.make_async_copy(src, dst, lsem.at[i])
        copy.start()
        return copy

    def rows(pos, first=0, count=st):
        return pl.ds(pos * st + first, count)

    own = [
        local(x_in, xg.at[rows(POS[0], 0, tb), pl.ds(0, dk)]),
        local(g_in, xg.at[rows(POS[0], 0, tb), pl.ds(dk, dk)]),
    ]
    weights = [local(u_in.at[:, pl.ds(q * fq, fq)], u.at[q]) for q in range(NX)]
    weights += [local(d_in.at[pl.ds(q * fq, fq), :], dn.at[q]) for q in range(NX)]

    barrier = pltpu.get_barrier_semaphore()
    partners = [(a, o) for a in "xy" for o in (1, 2, 3)] + [("z", o) for o in (1, 2, -1, -2)] + [("c", 1)]
    for axis, off in partners:
        pl.semaphore_signal(barrier, inc=1, device_id=device(axis, off), device_id_type=MESH)
    pl.semaphore_wait(barrier, len(partners))

    arrival, shared = {}, {}

    def pass_on(d, to, half, off):
        cols = pl.ds(half * dk, dk)
        arrival[to, half] = send(
            xg.at[rows(POS[d], 0, tb), cols], xg.at[rows(POS[to], 0, tb), cols], device("z", off)
        )

    def share(d):
        shared[d] = send(xg.at[rows(POS[d], 0, tb)], xg.at[rows(POS[d], tb, tb)], device("c", 1))

    for copy in own:
        copy.wait()
    for half in (0, 1):
        pass_on(0, -1, half, 1)
        pass_on(0, 1, half, -1)
    share(0)

    def arrive(d, half):
        arrival[d, half].wait_recv()
        if d in (-1, -2):
            pass_on(d, d - 1, half, 1)
        elif d in (1, 2):
            pass_on(d, d + 1, half, -1)
        elif (d, half) == (-3, 0):
            pass_on(d, 4, half, 1)
        elif (d, half) == (3, 1):
            pass_on(d, 4, half, -1)

    def arrive_first(d):
        arrive(d, 0)

    def arrive_second(d):
        if d == 4:
            arrive(d, 0)
        arrive(d, 1)
        share(d)

    def turn(_):
        for copy in weights:
            copy.wait()
        for q in range(NX):
            dt[q] = dn[q].T
            ut[q] = u[q].T

    pend, first = {}, {}
    low, high = pl.ds(0, fq), pl.ds(fq, fq)

    def axes(pos):
        return ("y", "x") if pos in Y_FIRST else ("x", "y")

    def around(pos):
        at = place[axes(pos)[0]]
        return at, (at + 1) % NX, (at + 2) % NX, (at + NX - 1) % NX

    def product(pos, q):
        part[q, rows(pos), :fq] = dot(xg[rows(pos), :dk], u[q], 1, 0).astype(bf16)
        part[q, rows(pos), fq:] = dot(xg[rows(pos), dk:], dt[q], 1, 0).astype(bf16)

    def far_products(pos):
        a1, _ = axes(pos)
        _, _, across, _ = around(pos)
        shared[ORDER[pos]].wait_recv()
        product(pos, across)
        first[pos] = [
            send(part.at[across, rows(pos), low], via.at[0, pos], device(a1, 1)),
            send(part.at[across, rows(pos), high], via.at[1, pos], device(a1, -1)),
        ]

    def near_products(pos):
        a1, _ = axes(pos)
        at, right, _, left = around(pos)
        product(pos, right)
        product(pos, left)
        pend[pos] = [
            send(part.at[right, rows(pos), high], full.at[0, pos, :, high], device(a1, 1)),
            send(part.at[left, rows(pos), low], full.at[1, pos, :, low], device(a1, -1)),
        ]
        product(pos, at)

    def first_sum(pos):
        a1, _ = axes(pos)
        _, right, _, left = around(pos)
        first[pos][0].wait_recv()
        part[right, rows(pos), :fq] = (
            part[right, rows(pos), :fq].astype(f32) + via[0, pos].astype(f32)
        ).astype(bf16)
        pend[pos].append(send(part.at[right, rows(pos), low], full.at[0, pos, :, low], device(a1, 1)))
        first[pos][1].wait_recv()
        part[left, rows(pos), fq:] = (
            part[left, rows(pos), fq:].astype(f32) + via[1, pos].astype(f32)
        ).astype(bf16)
        pend[pos].append(send(part.at[left, rows(pos), high], full.at[1, pos, :, high], device(a1, -1)))

    def second_sum(pos):
        a1, a2 = axes(pos)
        for copy in pend[pos]:
            copy.wait_recv()
        total = (
            part[place[a1], rows(pos), :].astype(f32) + full[0, pos].astype(f32) + full[1, pos].astype(f32)
        ).astype(bf16)
        for k in range(NX):
            quarter[pos, k] = total[k * sub:(k + 1) * sub]
        pend[pos] = [
            send(quarter.at[pos, (place[a2] + o) % NX], got.at[pos, o - 1], device(a2, o)) for o in (1, 3, 2)
        ]

    def act(pos):
        a1, a2 = axes(pos)
        for copy in pend[pos]:
            copy.wait_recv()
        total = quarter[pos, place[a2]].astype(f32)
        for o in range(NX - 1):
            total = total + got[pos, o].astype(f32)
        value, grad = activate(total[:, :fq], total[:, fq:])
        mine = pl.ds(pl.multiple_of(pos * st + place[a2] * sub, sub), sub)
        hid[place[a1], mine, :fq] = value
        hid[place[a1], mine, fq:] = grad
        block = hid.at[place[a1], mine]
        pend[pos] = [send(block, block, device(a2, o)) for o in (1, 3, 2)]

    def gather(pos):
        a1, _ = axes(pos)
        for copy in pend[pos]:
            copy.wait_recv()
        h = hid.at[place[a1], rows(pos), low]
        a = hid.at[place[a1], rows(pos), high]
        first[pos] = [send(h, h, device(a1, 1)), send(a, a, device(a1, -1))]
        pend[pos] = [send(a, a, device(a1, 1)), send(h, h, device(a1, -1))]

    def forward(pos):
        a1, _ = axes(pos)
        _, right, _, left = around(pos)
        first[pos][0].wait_recv()
        block = hid.at[left, rows(pos), low]
        pend[pos].append(send(block, block, device(a1, 1)))
        first[pos][1].wait_recv()
        block = hid.at[right, rows(pos), high]
        pend[pos].append(send(block, block, device(a1, -1)))

    whole = set()

    def complete(pos):
        if pos not in whole:
            whole.add(pos)
            for copy in pend[pos]:
                copy.wait_recv()

    def second_products(pos):
        complete(pos)
        out = dot(hid[0, rows(pos), :fq], dn[0], 1, 0)
        for q in range(1, NX):
            out = out + dot(hid[q, rows(pos), :fq], dn[q], 1, 0)
        outp[rows(pos), :dk] = out.astype(bf16)
        back = dot(hid[0, rows(pos), fq:], ut[0], 1, 0)
        for q in range(1, NX):
            back = back + dot(hid[q, rows(pos), fq:], ut[q], 1, 0)
        outp[rows(pos), dk:] = back.astype(bf16)
        pend[pos] = [send(outp.at[rows(pos, tb, tb)], sib.at[pos], device("c", 1))]

    def both_cores(pos):
        pend[pos][0].wait_recv()
        mine = rows(pos, 0, tb)
        total = outp[mine, :].astype(f32) + sib[pos].astype(f32)
        d = ORDER[pos]
        if d in (2, -2):
            side = 0 if d > 0 else 1
            far[3 if d > 0 else -3].wait_recv()
            far[4][side].wait_recv()
            total = total + mid[side].astype(f32)
            cols = slice(side * dk, side * dk + dk)
            outp[mine, :] = total.astype(bf16)
            outp[mine, cols] = (total[:, cols] + mid4[side].astype(f32)).astype(bf16)
        else:
            outp[mine, :] = total.astype(bf16)
        if d in (3, -3):
            far[d] = send(outp.at[mine], mid.at[0 if d > 0 else 1], device("z", d // 3))
        elif d == 4:
            far[4] = [
                send(outp.at[mine, pl.ds(0, dk)], mid4.at[0], device("z", 2)),
                send(outp.at[mine, pl.ds(dk, dk)], mid4.at[1], device("z", -2)),
            ]
        elif d:
            landed[d] = send(outp.at[mine], zbuf.at[ZSLOT[d]], device("z", d))

    far, landed = {}, {}

    def weight_grads(q):
        for pos in range(len(ORDER)):
            complete(pos)
        ug_o[:, q * fq:(q + 1) * fq] = dot(xg[:, :dk], hid[q, :, fq:], 0, 0).astype(bf16)
        dg_o[q * fq:(q + 1) * fq, :] = dot(hid[q, :, :fq], xg[:, dk:], 0, 0).astype(bf16)

    steps = {
        "aa": arrive_first, "arr": arrive_second, "tr": turn, "p1": far_products, "pb": near_products,
        "s1": first_sum, "s2": second_sum, "s3": act, "s4": gather, "s5": forward, "p2": second_products,
        "s6": both_cores, "dw": weight_grads,
    }
    for name, number in SCHEDULE:
        steps[name](number)

    total = outp[rows(POS[0], 0, tb), :].astype(f32)
    for d in (1, -1, 2, -2):
        landed[d].wait_recv()
        total = total + zbuf[ZSLOT[d]].astype(f32)
    out_o[...] = total[:, :dk].astype(bf16)
    back_o[...] = total[:, dk:].astype(bf16)
    for copy in sends:
        copy.wait_send()


def settle_kernel(*refs):
    n = len(refs) // 2
    copies = [pltpu.make_async_copy(refs[i], refs[n + i], refs[-1].at[i]) for i in range(n)]
    for copy in copies:
        copy.start()
    for copy in copies:
        copy.wait()


def settle(*arrays):
    n = len(arrays)
    return pl.pallas_call(
        settle_kernel,
        name="settle",
        out_shape=tuple(jax.ShapeDtypeStruct(a.shape, a.dtype) for a in arrays),
        in_specs=[pl.BlockSpec(memory_space=pltpu.VMEM)] * n,
        out_specs=(pl.BlockSpec(memory_space=pl.ANY),) * n,
        scratch_shapes=[pltpu.SemaphoreType.DMA((n,))],
        compiler_params=pltpu.CompilerParams(vmem_limit_bytes=16 * 2**20),
    )(*arrays)


def body(block_input, out_grad, up_weight, down_weight):
    tb, dk = block_input.shape
    f = up_weight.shape[1]
    fq, st, n = f // NX, 2 * tb, NZ
    vm = lambda *shape: pltpu.VMEM(shape, bf16)
    results = pl.pallas_call(
        kernel,
        name="block",
        out_shape=(vm(tb, dk), vm(tb, dk), vm(dk, f), vm(f, dk)),
        in_specs=[pl.BlockSpec(memory_space=pltpu.HBM)] * 4,
        out_specs=(pl.BlockSpec(memory_space=pltpu.VMEM),) * 4,
        scratch_shapes=[
            vm(n * st, 2 * dk),
            vm(NX, dk, fq),
            vm(NX, fq, dk),
            vm(NX, fq, dk),
            vm(NX, dk, fq),
            vm(NX, n * st, 2 * fq),
            vm(NX, n * st, 2 * fq),
            vm(2, n, st, fq),
            vm(2, n, st, 2 * fq),
            vm(n, NX, st // NX, 2 * fq),
            vm(n, NX - 1, st // NX, 2 * fq),
            vm(n * st, 2 * dk),
            vm(n, tb, 2 * dk),
            vm(4, tb, 2 * dk),
        vm(2, tb, 2 * dk),
        vm(2, tb, dk),
                pltpu.SemaphoreType.DMA((N_SEMS,)),
            pltpu.SemaphoreType.DMA((N_SEMS,)),
            pltpu.SemaphoreType.DMA((10,)),
        ],
        compiler_params=pltpu.CompilerParams(
            collective_id=0, has_side_effects=True, vmem_limit_bytes=40 * 2**20
        ),
        cost_estimate=pl.CostEstimate(flops=12 * n * st * dk * f, bytes_accessed=8 * dk * f, transcendentals=0),
    )(*(pltpu.with_memory_space_constraint(a, pltpu.HBM) for a in (block_input, out_grad, up_weight, down_weight)))
    return settle(*results)


def solution(mesh):
    return jax.shard_map(
        body,
        mesh=mesh,
        in_specs=(P("col", "row"), P("col", "row"), P("row", "col"), P("col", "row")),
        out_specs=(P("col", "row"), P("col", "row"), P("row", "col"), P("col", "row")),
        check_vma=False,
    )
```

```python
import functools

import jax
import jax.numpy as jnp
from jax import lax
from jax.experimental import pallas as pl
from jax.experimental.pallas import tpu as pltpu
from jax.sharding import PartitionSpec as P

MESH = pl.DeviceIdType.MESH
gelu_c = 0.7978845608028654
f32 = jnp.float32
bf16 = jnp.bfloat16

NX = 4
NZ = 8
ORDER = (0, 1, -1, 2, -2, 3, -3, 4)
Y_FIRST = (1, 2, 5, 7)
ZSLOT = {1: 0, -1: 1, 2: 2, -2: 3}
POS = {d: i for i, d in enumerate(ORDER)}
SCHEDULE = (
    ("tr", 0), ("aa", 1), ("aa", -1), ("p1", 0), ("arr", 1), ("arr", -1), ("aa", 2), ("p1", 1),
    ("aa", -2), ("pb", 0), ("arr", 2), ("p1", 2), ("arr", -2), ("s1", 0), ("pb", 2), ("pb", 1),
    ("p1", 3), ("pb", 3), ("s1", 1), ("aa", -3), ("aa", 3), ("p1", 4), ("arr", 3), ("arr", -3),
    ("p1", 5), ("p1", 6), ("s1", 2), ("pb", 6), ("pb", 5), ("arr", 4), ("pb", 4), ("p1", 7),
    ("s1", 6), ("s1", 3), ("s1", 5), ("pb", 7), ("s1", 4), ("s2", 1), ("s1", 7), ("s2", 6),
    ("s2", 5), ("s2", 2), ("s2", 4), ("s2", 3), ("s2", 7), ("s3", 6), ("s2", 0), ("s3", 5),
    ("s3", 1), ("s3", 4), ("s3", 7), ("s3", 3), ("s4", 6), ("s4", 5), ("s4", 4), ("s4", 7),
    ("s5", 6), ("s4", 3), ("s3", 2), ("s5", 5), ("s5", 7), ("s4", 1), ("s5", 4), ("s3", 0),
    ("p2", 6), ("s5", 3), ("p2", 5), ("s6", 6), ("p2", 7), ("s5", 1), ("s6", 7), ("s4", 2),
    ("s6", 5), ("s4", 0), ("p2", 4), ("p2", 1), ("s5", 2), ("p2", 3), ("s6", 1), ("s5", 0),
    ("s6", 4), ("s6", 3), ("p2", 2), ("dw", 0), ("s6", 2), ("p2", 0), ("dw", 1), ("dw", 2),
    ("s6", 0), ("dw", 3),
)
N_SEMS = 224


def activate(preact, hgrad):
    cubed = preact * preact * preact
    tanh_term = jnp.tanh(gelu_c * (preact + 0.044715 * cubed))
    value = 0.5 * preact * (1.0 + tanh_term)
    slope = 0.5 * (1.0 + tanh_term) + 0.5 * preact * (1.0 - tanh_term * tanh_term) * gelu_c * (
        1.0 + 3.0 * 0.044715 * preact * preact
    )
    return value.astype(bf16), (hgrad * slope).astype(bf16)


def dot(a, b, ca, cb):
    return lax.dot_general(a, b, (((ca,), (cb,)), ((), ())), preferred_element_type=f32)


def kernel(
    x_in, g_in, u_in, d_in,
    out_o, back_o, ug_o, dg_o,
    xg, u, dn, ut, dt, part, hid, via, full, quarter, got, outp, sib, zbuf, mid, mid4,
    ssem, rsem, lsem,
):
    tb, dk = x_in.shape
    fq = u.shape[2]
    st = 2 * tb
    sub = st // NX
    row, col = lax.axis_index("row"), lax.axis_index("col")
    cx, cy = row % NX, row // NX
    cz, core = col // 2, col % 2

    def device(axis, off):
        if axis == "x":
            return (cy * NX + (cx + off) % NX, col)
        if axis == "y":
            return (((cy + off) % NX) * NX + cx, col)
        if axis == "z":
            return (row, ((cz + off + NZ) % NZ) * 2 + core)
        return (row, cz * 2 + 1 - core)

    place = {"x": cx, "y": cy}
    sends = []
    n_local = [0]

    def send(src, dst, target):
        i = len(sends)
        copy = pltpu.make_async_remote_copy(
            src_ref=src, dst_ref=dst, send_sem=ssem.at[i], recv_sem=rsem.at[i],
            device_id=target, device_id_type=MESH,
        )
        copy.start()
        sends.append(copy)
        return copy

    def local(src, dst):
        i = n_local[0]
        n_local[0] += 1
        copy = pltpu.make_async_copy(src, dst, lsem.at[i])
        copy.start()
        return copy

    def rows(pos, first=0, count=st):
        return pl.ds(pos * st + first, count)

    barrier = pltpu.get_barrier_semaphore()
    partners = [("z", 1), ("z", -1), ("c", 1)] + [(a, o) for a in "xy" for o in (1, 3, 2)] + [("z", 2), ("z", -2)]
    for axis, off in partners:
        pl.semaphore_signal(barrier, inc=1, device_id=device(axis, off), device_id_type=MESH)
    own = [
        local(x_in, xg.at[rows(POS[0], 0, tb), pl.ds(0, dk)]),
        local(g_in, xg.at[rows(POS[0], 0, tb), pl.ds(dk, dk)]),
    ]
    weights = [local(u_in.at[:, pl.ds(q * fq, fq)], u.at[q]) for q in range(NX)]
    weights += [local(d_in.at[pl.ds(q * fq, fq), :], dn.at[q]) for q in range(NX)]

    pl.semaphore_wait(barrier, len(partners))

    arrival, shared = {}, {}

    def pass_on(d, to, half, off):
        cols = pl.ds(half * dk, dk)
        source = xg.at[rows(POS[d], 0, tb), cols] if d else (x_in, g_in)[half]
        arrival[to, half] = send(source, xg.at[rows(POS[to], 0, tb), cols], device("z", off))

    def share(d):
        shared[d] = send(xg.at[rows(POS[d], 0, tb)], xg.at[rows(POS[d], tb, tb)], device("c", 1))

    for half in (0, 1):
        pass_on(0, -1, half, 1)
        pass_on(0, 1, half, -1)
    for copy in own:
        copy.wait()
    share(0)

    def arrive(d, half):
        arrival[d, half].wait_recv()
        if d in (-1, -2):
            pass_on(d, d - 1, half, 1)
        elif d in (1, 2):
            pass_on(d, d + 1, half, -1)
        elif (d, half) == (-3, 0):
            pass_on(d, 4, half, 1)
        elif (d, half) == (3, 1):
            pass_on(d, 4, half, -1)

    def arrive_first(d):
        arrive(d, 0)

    def arrive_second(d):
        if d == 4:
            arrive(d, 0)
        arrive(d, 1)
        share(d)

    def turn(_):
        for copy in weights:
            copy.wait()
        for q in range(NX):
            dt[q] = dn[q].T
            ut[q] = u[q].T

    pend, first = {}, {}
    low, high = pl.ds(0, fq), pl.ds(fq, fq)

    def axes(pos):
        return ("y", "x") if pos in Y_FIRST else ("x", "y")

    def around(pos):
        at = place[axes(pos)[0]]
        return at, (at + 1) % NX, (at + 2) % NX, (at + NX - 1) % NX

    def product(pos, q):
        part[q, rows(pos), :fq] = dot(xg[rows(pos), :dk], u[q], 1, 0).astype(bf16)
        part[q, rows(pos), fq:] = dot(xg[rows(pos), dk:], dt[q], 1, 0).astype(bf16)

    def far_products(pos):
        a1, _ = axes(pos)
        _, _, across, _ = around(pos)
        shared[ORDER[pos]].wait_recv()
        product(pos, across)
        first[pos] = [
            send(part.at[across, rows(pos), low], via.at[0, pos], device(a1, 1)),
            send(part.at[across, rows(pos), high], via.at[1, pos], device(a1, -1)),
        ]

    def near_products(pos):
        a1, _ = axes(pos)
        at, right, _, left = around(pos)
        product(pos, right)
        product(pos, left)
        pend[pos] = [
            send(part.at[right, rows(pos), high], full.at[0, pos, :, high], device(a1, 1)),
            send(part.at[left, rows(pos), low], full.at[1, pos, :, low], device(a1, -1)),
        ]
        product(pos, at)

    def first_sum(pos):
        a1, _ = axes(pos)
        _, right, _, left = around(pos)
        first[pos][0].wait_recv()
        part[right, rows(pos), :fq] = (
            part[right, rows(pos), :fq].astype(f32) + via[0, pos].astype(f32)
        ).astype(bf16)
        pend[pos].append(send(part.at[right, rows(pos), low], full.at[0, pos, :, low], device(a1, 1)))
        first[pos][1].wait_recv()
        part[left, rows(pos), fq:] = (
            part[left, rows(pos), fq:].astype(f32) + via[1, pos].astype(f32)
        ).astype(bf16)
        pend[pos].append(send(part.at[left, rows(pos), high], full.at[1, pos, :, high], device(a1, -1)))

    def second_sum(pos):
        a1, a2 = axes(pos)
        for copy in pend[pos]:
            copy.wait_recv()
        total = (
            part[place[a1], rows(pos), :].astype(f32) + full[0, pos].astype(f32) + full[1, pos].astype(f32)
        ).astype(bf16)
        for k in range(NX):
            quarter[pos, k] = total[k * sub:(k + 1) * sub]
        pend[pos] = [
            send(quarter.at[pos, (place[a2] + o) % NX], got.at[pos, o - 1], device(a2, o)) for o in (2, 1, 3)
        ]

    def act(pos):
        a1, a2 = axes(pos)
        for copy in pend[pos]:
            copy.wait_recv()
        total = quarter[pos, place[a2]].astype(f32)
        for o in range(NX - 1):
            total = total + got[pos, o].astype(f32)
        value, grad = activate(total[:, :fq], total[:, fq:])
        mine = pl.ds(pl.multiple_of(pos * st + place[a2] * sub, sub), sub)
        hid[place[a1], mine, :fq] = value
        hid[place[a1], mine, fq:] = grad
        block = hid.at[place[a1], mine]
        pend[pos] = [send(block, block, device(a2, o)) for o in (2, 1, 3)]

    def gather(pos):
        a1, _ = axes(pos)
        for copy in pend[pos]:
            copy.wait_recv()
        h = hid.at[place[a1], rows(pos), low]
        a = hid.at[place[a1], rows(pos), high]
        first[pos] = [send(h, h, device(a1, 1)), send(a, a, device(a1, -1))]
        pend[pos] = [send(a, a, device(a1, 1)), send(h, h, device(a1, -1))]

    def forward(pos):
        a1, _ = axes(pos)
        _, right, _, left = around(pos)
        first[pos][0].wait_recv()
        block = hid.at[left, rows(pos), low]
        pend[pos].append(send(block, block, device(a1, 1)))
        first[pos][1].wait_recv()
        block = hid.at[right, rows(pos), high]
        pend[pos].append(send(block, block, device(a1, -1)))

    whole = set()

    def complete(pos):
        if pos not in whole:
            whole.add(pos)
            for copy in pend[pos]:
                copy.wait_recv()

    def second_products(pos):
        complete(pos)
        out = dot(hid[0, rows(pos), :fq], dn[0], 1, 0)
        for q in range(1, NX):
            out = out + dot(hid[q, rows(pos), :fq], dn[q], 1, 0)
        outp[rows(pos), :dk] = out.astype(bf16)
        back = dot(hid[0, rows(pos), fq:], ut[0], 1, 0)
        for q in range(1, NX):
            back = back + dot(hid[q, rows(pos), fq:], ut[q], 1, 0)
        outp[rows(pos), dk:] = back.astype(bf16)
        pend[pos] = [send(outp.at[rows(pos, tb, tb)], sib.at[pos], device("c", 1))]

    def both_cores(pos):
        pend[pos][0].wait_recv()
        mine = rows(pos, 0, tb)
        total = outp[mine, :].astype(f32) + sib[pos].astype(f32)
        d = ORDER[pos]
        if d in (2, -2):
            side = 0 if d > 0 else 1
            far[3 if d > 0 else -3].wait_recv()
            far[4][side].wait_recv()
            total = total + mid[side].astype(f32)
            cols = slice(side * dk, side * dk + dk)
            outp[mine, :] = total.astype(bf16)
            outp[mine, cols] = (total[:, cols] + mid4[side].astype(f32)).astype(bf16)
        else:
            outp[mine, :] = total.astype(bf16)
        if d in (3, -3):
            far[d] = send(outp.at[mine], mid.at[0 if d > 0 else 1], device("z", d // 3))
        elif d == 4:
            far[4] = [
                send(outp.at[mine, pl.ds(0, dk)], mid4.at[0], device("z", 2)),
                send(outp.at[mine, pl.ds(dk, dk)], mid4.at[1], device("z", -2)),
            ]
        elif d:
            landed[d] = send(outp.at[mine], zbuf.at[ZSLOT[d]], device("z", d))

    far, landed = {}, {}

    def weight_grads(q):
        for pos in range(len(ORDER)):
            complete(pos)
        ug_o[:, q * fq:(q + 1) * fq] = dot(xg[:, :dk], hid[q, :, fq:], 0, 0).astype(bf16)
        dg_o[q * fq:(q + 1) * fq, :] = dot(hid[q, :, :fq], xg[:, dk:], 0, 0).astype(bf16)

    steps = {
        "aa": arrive_first, "arr": arrive_second, "tr": turn, "p1": far_products, "pb": near_products,
        "s1": first_sum, "s2": second_sum, "s3": act, "s4": gather, "s5": forward, "p2": second_products,
        "s6": both_cores, "dw": weight_grads,
    }
    for name, number in SCHEDULE:
        steps[name](number)

    last = [landed[d] for d in (1, -2, 2, -1)]
    for copy in sends:
        if all(copy is not other for other in last):
            copy.wait_send()
    total = outp[rows(POS[0], 0, tb), :].astype(f32)
    for d in (1, -2, 2, -1):
        landed[d].wait_recv()
        total = total + zbuf[ZSLOT[d]].astype(f32)
    out_o[...] = total[:, :dk].astype(bf16)
    back_o[...] = total[:, dk:].astype(bf16)
    for copy in last:
        copy.wait_send()


def settle_kernel(*refs):
    n = len(refs) // 2
    copies = [pltpu.make_async_copy(refs[i], refs[n + i], refs[-1].at[i]) for i in range(n)]
    for copy in copies:
        copy.start()
    for copy in copies:
        copy.wait()


def settle(*arrays):
    n = len(arrays)
    return pl.pallas_call(
        settle_kernel,
        name="settle",
        out_shape=tuple(jax.ShapeDtypeStruct(a.shape, a.dtype) for a in arrays),
        in_specs=[pl.BlockSpec(memory_space=pltpu.VMEM)] * n,
        out_specs=(pl.BlockSpec(memory_space=pl.ANY),) * n,
        scratch_shapes=[pltpu.SemaphoreType.DMA((n,))],
        compiler_params=pltpu.CompilerParams(vmem_limit_bytes=16 * 2**20),
    )(*arrays)


def body(block_input, out_grad, up_weight, down_weight):
    tb, dk = block_input.shape
    f = up_weight.shape[1]
    fq, st, n = f // NX, 2 * tb, NZ
    vm = lambda *shape: pltpu.VMEM(shape, bf16)
    results = pl.pallas_call(
        kernel,
        name="block",
        out_shape=(vm(tb, dk), vm(tb, dk), vm(dk, f), vm(f, dk)),
        in_specs=[pl.BlockSpec(memory_space=pltpu.HBM)] * 4,
        out_specs=(pl.BlockSpec(memory_space=pltpu.VMEM),) * 4,
        scratch_shapes=[
            vm(n * st, 2 * dk),
            vm(NX, dk, fq),
            vm(NX, fq, dk),
            vm(NX, fq, dk),
            vm(NX, dk, fq),
            vm(NX, n * st, 2 * fq),
            vm(NX, n * st, 2 * fq),
            vm(2, n, st, fq),
            vm(2, n, st, 2 * fq),
            vm(n, NX, st // NX, 2 * fq),
            vm(n, NX - 1, st // NX, 2 * fq),
            vm(n * st, 2 * dk),
            vm(n, tb, 2 * dk),
            vm(4, tb, 2 * dk),
        vm(2, tb, 2 * dk),
        vm(2, tb, dk),
                pltpu.SemaphoreType.DMA((N_SEMS,)),
            pltpu.SemaphoreType.DMA((N_SEMS,)),
            pltpu.SemaphoreType.DMA((10,)),
        ],
        compiler_params=pltpu.CompilerParams(
            collective_id=0, has_side_effects=True, vmem_limit_bytes=40 * 2**20
        ),
        cost_estimate=pl.CostEstimate(flops=12 * n * st * dk * f, bytes_accessed=8 * dk * f, transcendentals=0),
    )(*(pltpu.with_memory_space_constraint(a, pltpu.HBM) for a in (block_input, out_grad, up_weight, down_weight)))
    return settle(*results)


def solution(mesh):
    return jax.shard_map(
        body,
        mesh=mesh,
        in_specs=(P("col", "row"), P("col", "row"), P("row", "col"), P("col", "row")),
        out_specs=(P("col", "row"), P("col", "row"), P("row", "col"), P("col", "row")),
        check_vma=False,
    )
```

```python
import functools

import jax
import jax.numpy as jnp
from jax import lax
from jax.experimental import pallas as pl
from jax.experimental.pallas import tpu as pltpu
from jax.sharding import PartitionSpec as P

MESH = pl.DeviceIdType.MESH
gelu_c = 0.7978845608028654
f32 = jnp.float32
bf16 = jnp.bfloat16

NX = 4
NZ = 8
ORDER = (0, 1, -1, 2, -2, 3, -3, 4)
Y_FIRST = (1, 2, 5, 7)
ZSLOT = {1: 0, -1: 1, 2: 2, -2: 3}
POS = {d: i for i, d in enumerate(ORDER)}
SCHEDULE = (
    ("tr", 0), ("aa", 1), ("aa", -1), ("p1", 0), ("arr", 1), ("arr", -1), ("aa", 2), ("p1", 1),
    ("aa", -2), ("pb", 0), ("arr", 2), ("p1", 2), ("arr", -2), ("s1", 0), ("pb", 2), ("pb", 1),
    ("p1", 3), ("pb", 3), ("s1", 1), ("aa", -3), ("aa", 3), ("p1", 4), ("arr", 3), ("arr", -3),
    ("p1", 5), ("p1", 6), ("s1", 2), ("pb", 6), ("pb", 5), ("arr", 4), ("pb", 4), ("p1", 7),
    ("s1", 6), ("s1", 3), ("s1", 5), ("pb", 7), ("s1", 4), ("s2", 1), ("s1", 7), ("s2", 6),
    ("s2", 5), ("s2", 2), ("s2", 4), ("s2", 3), ("s2", 7), ("s3", 6), ("s2", 0), ("s3", 5),
    ("s3", 1), ("s3", 4), ("s3", 7), ("s3", 3), ("s4", 6), ("s4", 5), ("s4", 4), ("s4", 7),
    ("s5", 6), ("s4", 3), ("s3", 2), ("s5", 5), ("s5", 7), ("s4", 1), ("s5", 4), ("s3", 0),
    ("p2", 6), ("s5", 3), ("p2", 5), ("s6", 6), ("p2", 7), ("s5", 1), ("s6", 7), ("s4", 2),
    ("s6", 5), ("s4", 0), ("p2", 4), ("p2", 1), ("s5", 2), ("p2", 3), ("s6", 1), ("s5", 0),
    ("s6", 4), ("s6", 3), ("p2", 2), ("dw", 0), ("s6", 2), ("p2", 0), ("dw", 1), ("dw", 2),
    ("s6", 0), ("dw", 3),
)
N_SEMS = 224


def activate(preact, hgrad):
    cubed = preact * preact * preact
    tanh_term = jnp.tanh(gelu_c * (preact + 0.044715 * cubed))
    value = 0.5 * preact * (1.0 + tanh_term)
    slope = 0.5 * (1.0 + tanh_term) + 0.5 * preact * (1.0 - tanh_term * tanh_term) * gelu_c * (
        1.0 + 3.0 * 0.044715 * preact * preact
    )
    return value.astype(bf16), (hgrad * slope).astype(bf16)


def dot(a, b, ca, cb):
    return lax.dot_general(a, b, (((ca,), (cb,)), ((), ())), preferred_element_type=f32)


def kernel(
    x_in, g_in, u_in, d_in,
    out_o, back_o, ug_o, dg_o,
    xg, u, dn, ut, dt, part, hid, via, full, quarter, got, outp, sib, zbuf, mid, mid4,
    ssem, rsem, lsem,
):
    tb, dk = x_in.shape
    fq = u.shape[2]
    st = 2 * tb
    sub = st // NX
    row, col = lax.axis_index("row"), lax.axis_index("col")
    cx, cy = row % NX, row // NX
    cz, core = col // 2, col % 2

    def device(axis, off):
        if axis == "x":
            return (cy * NX + (cx + off) % NX, col)
        if axis == "y":
            return (((cy + off) % NX) * NX + cx, col)
        if axis == "z":
            return (row, ((cz + off + NZ) % NZ) * 2 + core)
        return (row, cz * 2 + 1 - core)

    place = {"x": cx, "y": cy}
    sends = []
    n_local = [0]

    def send(src, dst, target):
        i = len(sends)
        copy = pltpu.make_async_remote_copy(
            src_ref=src, dst_ref=dst, send_sem=ssem.at[i], recv_sem=rsem.at[i],
            device_id=target, device_id_type=MESH,
        )
        copy.start()
        sends.append(copy)
        return copy

    def local(src, dst):
        i = n_local[0]
        n_local[0] += 1
        copy = pltpu.make_async_copy(src, dst, lsem.at[i])
        copy.start()
        return copy

    def rows(pos, first=0, count=st):
        return pl.ds(pos * st + first, count)

    own = [
        local(x_in, xg.at[rows(POS[0], 0, tb), pl.ds(0, dk)]),
        local(g_in, xg.at[rows(POS[0], 0, tb), pl.ds(dk, dk)]),
    ]
    weights = [local(u_in.at[:, pl.ds(q * fq, fq)], u.at[q]) for q in range(NX)]
    weights += [local(d_in.at[pl.ds(q * fq, fq), :], dn.at[q]) for q in range(NX)]

    barrier = pltpu.get_barrier_semaphore()
    partners = [(a, o) for a in "xy" for o in (1, 2, 3)] + [("z", o) for o in (1, 2, -1, -2)] + [("c", 1)]
    for axis, off in partners:
        pl.semaphore_signal(barrier, inc=1, device_id=device(axis, off), device_id_type=MESH)
    pl.semaphore_wait(barrier, len(partners))

    arrival, shared = {}, {}

    def pass_on(d, to, half, off):
        cols = pl.ds(half * dk, dk)
        arrival[to, half] = send(
            xg.at[rows(POS[d], 0, tb), cols], xg.at[rows(POS[to], 0, tb), cols], device("z", off)
        )

    def share(d):
        shared[d] = send(xg.at[rows(POS[d], 0, tb)], xg.at[rows(POS[d], tb, tb)], device("c", 1))

    for copy in own:
        copy.wait()
    for half in (0, 1):
        pass_on(0, -1, half, 1)
        pass_on(0, 1, half, -1)
    share(0)

    def arrive(d, half):
        arrival[d, half].wait_recv()
        if d in (-1, -2):
            pass_on(d, d - 1, half, 1)
        elif d in (1, 2):
            pass_on(d, d + 1, half, -1)
        elif (d, half) == (-3, 0):
            pass_on(d, 4, half, 1)
        elif (d, half) == (3, 1):
            pass_on(d, 4, half, -1)

    def arrive_first(d):
        arrive(d, 0)

    def arrive_second(d):
        if d == 4:
            arrive(d, 0)
        arrive(d, 1)
        share(d)

    def turn(_):
        for copy in weights:
            copy.wait()
        for q in range(NX):
            dt[q] = dn[q].T
            ut[q] = u[q].T

    pend, first = {}, {}
    low, high = pl.ds(0, fq), pl.ds(fq, fq)

    def axes(pos):
        return ("y", "x") if pos in Y_FIRST else ("x", "y")

    def around(pos):
        at = place[axes(pos)[0]]
        return at, (at + 1) % NX, (at + 2) % NX, (at + NX - 1) % NX

    def product(pos, q):
        part[q, rows(pos), :fq] = dot(xg[rows(pos), :dk], u[q], 1, 0).astype(bf16)
        part[q, rows(pos), fq:] = dot(xg[rows(pos), dk:], dt[q], 1, 0).astype(bf16)

    def far_products(pos):
        a1, _ = axes(pos)
        _, _, across, _ = around(pos)
        shared[ORDER[pos]].wait_recv()
        product(pos, across)
        first[pos] = [
            send(part.at[across, rows(pos), low], via.at[0, pos], device(a1, 1)),
            send(part.at[across, rows(pos), high], via.at[1, pos], device(a1, -1)),
        ]

    def near_products(pos):
        a1, _ = axes(pos)
        at, right, _, left = around(pos)
        product(pos, right)
        product(pos, left)
        pend[pos] = [
            send(part.at[right, rows(pos), high], full.at[0, pos, :, high], device(a1, 1)),
            send(part.at[left, rows(pos), low], full.at[1, pos, :, low], device(a1, -1)),
        ]
        product(pos, at)

    def first_sum(pos):
        a1, _ = axes(pos)
        _, right, _, left = around(pos)
        first[pos][0].wait_recv()
        part[right, rows(pos), :fq] = (
            part[right, rows(pos), :fq].astype(f32) + via[0, pos].astype(f32)
        ).astype(bf16)
        pend[pos].append(send(part.at[right, rows(pos), low], full.at[0, pos, :, low], device(a1, 1)))
        first[pos][1].wait_recv()
        part[left, rows(pos), fq:] = (
            part[left, rows(pos), fq:].astype(f32) + via[1, pos].astype(f32)
        ).astype(bf16)
        pend[pos].append(send(part.at[left, rows(pos), high], full.at[1, pos, :, high], device(a1, -1)))

    def second_sum(pos):
        a1, a2 = axes(pos)
        for copy in pend[pos]:
            copy.wait_recv()
        total = (
            part[place[a1], rows(pos), :].astype(f32) + full[0, pos].astype(f32) + full[1, pos].astype(f32)
        ).astype(bf16)
        for k in range(NX):
            quarter[pos, k] = total[k * sub:(k + 1) * sub]
        pend[pos] = [
            send(quarter.at[pos, (place[a2] + o) % NX], got.at[pos, o - 1], device(a2, o)) for o in (1, 3, 2)
        ]

    def act(pos):
        a1, a2 = axes(pos)
        for copy in pend[pos]:
            copy.wait_recv()
        total = quarter[pos, place[a2]].astype(f32)
        for o in range(NX - 1):
            total = total + got[pos, o].astype(f32)
        value, grad = activate(total[:, :fq], total[:, fq:])
        mine = pl.ds(pl.multiple_of(pos * st + place[a2] * sub, sub), sub)
        hid[place[a1], mine, :fq] = value
        hid[place[a1], mine, fq:] = grad
        block = hid.at[place[a1], mine]
        pend[pos] = [send(block, block, device(a2, o)) for o in (1, 3, 2)]

    def gather(pos):
        a1, _ = axes(pos)
        for copy in pend[pos]:
            copy.wait_recv()
        h = hid.at[place[a1], rows(pos), low]
        a = hid.at[place[a1], rows(pos), high]
        first[pos] = [send(h, h, device(a1, 1)), send(a, a, device(a1, -1))]
        pend[pos] = [send(a, a, device(a1, 1)), send(h, h, device(a1, -1))]

    def forward(pos):
        a1, _ = axes(pos)
        _, right, _, left = around(pos)
        first[pos][0].wait_recv()
        block = hid.at[left, rows(pos), low]
        pend[pos].append(send(block, block, device(a1, 1)))
        first[pos][1].wait_recv()
        block = hid.at[right, rows(pos), high]
        pend[pos].append(send(block, block, device(a1, -1)))

    whole = set()

    def complete(pos):
        if pos not in whole:
            whole.add(pos)
            for copy in pend[pos]:
                copy.wait_recv()

    def second_products(pos):
        complete(pos)
        out = dot(hid[0, rows(pos), :fq], dn[0], 1, 0)
        for q in range(1, NX):
            out = out + dot(hid[q, rows(pos), :fq], dn[q], 1, 0)
        outp[rows(pos), :dk] = out.astype(bf16)
        pend[pos] = [send(outp.at[rows(pos, tb, tb), pl.ds(0, dk)], sib.at[pos, :, pl.ds(0, dk)], device("c", 1))]
        back = dot(hid[0, rows(pos), fq:], ut[0], 1, 0)
        for q in range(1, NX):
            back = back + dot(hid[q, rows(pos), fq:], ut[q], 1, 0)
        outp[rows(pos), dk:] = back.astype(bf16)
        pend[pos].append(
            send(outp.at[rows(pos, tb, tb), pl.ds(dk, dk)], sib.at[pos, :, pl.ds(dk, dk)], device("c", 1))
        )

    def both_cores(pos):
        mine = rows(pos, 0, tb)
        d = ORDER[pos]
        side = 0 if d > 0 else 1
        for half in (0, 1):
            cols, span = slice(half * dk, half * dk + dk), pl.ds(half * dk, dk)
            pend[pos][half].wait_recv()
            total = outp[mine, cols].astype(f32) + sib[pos, :, cols].astype(f32)
            if d in (2, -2):
                far[3 if d > 0 else -3][half].wait_recv()
                total = total + mid[side, :, cols].astype(f32)
                if half == side:
                    far[4][side].wait_recv()
                    total = total + mid4[side].astype(f32)
            outp[mine, cols] = total.astype(bf16)
            block = outp.at[mine, span]
            if d in (3, -3):
                far.setdefault(d, []).append(send(block, mid.at[side, :, span], device("z", d // 3)))
            elif d == 4:
                far.setdefault(d, []).append(send(block, mid4.at[half], device("z", 2 if half == 0 else -2)))
            elif d:
                landed.setdefault(d, []).append(send(block, zbuf.at[ZSLOT[d], :, span], device("z", d)))

    far, landed = {}, {}

    def weight_grads(q):
        for pos in range(len(ORDER)):
            complete(pos)
        ug_o[:, q * fq:(q + 1) * fq] = dot(xg[:, :dk], hid[q, :, fq:], 0, 0).astype(bf16)
        dg_o[q * fq:(q + 1) * fq, :] = dot(hid[q, :, :fq], xg[:, dk:], 0, 0).astype(bf16)

    steps = {
        "aa": arrive_first, "arr": arrive_second, "tr": turn, "p1": far_products, "pb": near_products,
        "s1": first_sum, "s2": second_sum, "s3": act, "s4": gather, "s5": forward, "p2": second_products,
        "s6": both_cores, "dw": weight_grads,
    }
    for name, number in SCHEDULE:
        steps[name](number)

    total = outp[rows(POS[0], 0, tb), :].astype(f32)
    for d in (1, -1, 2, -2):
        for copy in landed[d]:
            copy.wait_recv()
        total = total + zbuf[ZSLOT[d]].astype(f32)
    out_o[...] = total[:, :dk].astype(bf16)
    back_o[...] = total[:, dk:].astype(bf16)
    for copy in sends:
        copy.wait_send()


def settle_kernel(*refs):
    n = len(refs) // 2
    copies = [pltpu.make_async_copy(refs[i], refs[n + i], refs[-1].at[i]) for i in range(n)]
    for copy in copies:
        copy.start()
    for copy in copies:
        copy.wait()


def settle(*arrays):
    n = len(arrays)
    return pl.pallas_call(
        settle_kernel,
        name="settle",
        out_shape=tuple(jax.ShapeDtypeStruct(a.shape, a.dtype) for a in arrays),
        in_specs=[pl.BlockSpec(memory_space=pltpu.VMEM)] * n,
        out_specs=(pl.BlockSpec(memory_space=pl.ANY),) * n,
        scratch_shapes=[pltpu.SemaphoreType.DMA((n,))],
        compiler_params=pltpu.CompilerParams(vmem_limit_bytes=16 * 2**20),
    )(*arrays)


def body(block_input, out_grad, up_weight, down_weight):
    tb, dk = block_input.shape
    f = up_weight.shape[1]
    fq, st, n = f // NX, 2 * tb, NZ
    vm = lambda *shape: pltpu.VMEM(shape, bf16)
    results = pl.pallas_call(
        kernel,
        name="block",
        out_shape=(vm(tb, dk), vm(tb, dk), vm(dk, f), vm(f, dk)),
        in_specs=[pl.BlockSpec(memory_space=pltpu.HBM)] * 4,
        out_specs=(pl.BlockSpec(memory_space=pltpu.VMEM),) * 4,
        scratch_shapes=[
            vm(n * st, 2 * dk),
            vm(NX, dk, fq),
            vm(NX, fq, dk),
            vm(NX, fq, dk),
            vm(NX, dk, fq),
            vm(NX, n * st, 2 * fq),
            vm(NX, n * st, 2 * fq),
            vm(2, n, st, fq),
            vm(2, n, st, 2 * fq),
            vm(n, NX, st // NX, 2 * fq),
            vm(n, NX - 1, st // NX, 2 * fq),
            vm(n * st, 2 * dk),
            vm(n, tb, 2 * dk),
            vm(4, tb, 2 * dk),
        vm(2, tb, 2 * dk),
        vm(2, tb, dk),
                pltpu.SemaphoreType.DMA((N_SEMS,)),
            pltpu.SemaphoreType.DMA((N_SEMS,)),
            pltpu.SemaphoreType.DMA((10,)),
        ],
        compiler_params=pltpu.CompilerParams(
            collective_id=0, has_side_effects=True, vmem_limit_bytes=40 * 2**20
        ),
        cost_estimate=pl.CostEstimate(flops=12 * n * st * dk * f, bytes_accessed=8 * dk * f, transcendentals=0),
    )(*(pltpu.with_memory_space_constraint(a, pltpu.HBM) for a in (block_input, out_grad, up_weight, down_weight)))
    return settle(*results)


def solution(mesh):
    return jax.shard_map(
        body,
        mesh=mesh,
        in_specs=(P("col", "row"), P("col", "row"), P("row", "col"), P("col", "row")),
        out_specs=(P("col", "row"), P("col", "row"), P("row", "col"), P("col", "row")),
        check_vma=False,
    )
```
